512 devices in a mesh: fsdp: 64 (over y, z), store: 8 (over x, core).
Axes of the slice: x: 4, y: 8, z: 8, core: 2. Of those that a mesh axis runs over, the one named last changes fastest.
Arguments:
- layer_input: bfloat16 [16384, 5120], P('fsdp', 'store'), may hold values from -6 to 6
- gate_pre: bfloat16 [16384, 13824], P('fsdp', 'store'), may hold values from -6 to 6
- up_pre: bfloat16 [16384, 13824], P('fsdp', 'store'), may hold values from -6 to 6
- hidden_grad: bfloat16 [16384, 13824], P('fsdp', 'store'), may hold values from -6 to 6
- out_grad: bfloat16 [16384, 5120], P('fsdp', 'store'), may hold values from -6 to 6
- proj_model_in: bfloat16 [5120, 128], P('store'), may hold values from -0.078125 to 0.078125
- proj_hidden_in: bfloat16 [13824, 64], P('store'), may hold values from -0.0546875 to 0.0546875
- proj_hidden_out: bfloat16 [13824, 128], P('store'), may hold values from -0.0546875 to 0.0546875
- proj_model_out: bfloat16 [5120, 64], P('store'), may hold values from -0.078125 to 0.078125
- queries: bfloat16 [8192, 3, 4096], P('fsdp', None, 'store'), may hold values from -0.0546875 to 0.0546875
- validity: int32 [128, 128], P('fsdp'), may hold values 0 or 1
- owners: int32 [128], replicated, may hold values from 0 to 63, as said below
Outputs:
- scores: float32 [128, 8192], P('store', 'fsdp')
- stored: bfloat16 [256, 3, 4096], P('fsdp', None, 'store')
The draws below stay inside these ranges and needn't reach their ends.
Inputs may be any that keep to these rules, and one draw needn't show every extreme that they name: `owners`: each owner owns at most 4 sequences, and some owner owns exactly 4.
All inputs are finite; a program needn't handle non-finite values. No bound on the sum of `validity` on one device may be relied on, other than what follows from the above.
Results may differ from the reference program's by a relative error of at most 0.0049.
Values may be sent and summed in bfloat16 or wider, within the bound.
No kernel may reach another device: no remote copies, remote signals or barrier semaphores. Data moves between devices by JAX's collectives and lax.ppermute only.
A program may use at most 64 MiB of HBM per device.

```python
import jax
import jax.numpy as jnp
from jax import lax

D = 5120
FF = 13824
RANK = 64
LEN = 128
SEQ_DEV = 2
OWNERS = 64
EXAMPLES = 128
TOKENS = 16384
CAP = 4
NQ = 8192


def draw_owners(key, part):
    key = jax.random.fold_in(key, 11)
    key_moves, key_order, key_shuffle = jax.random.split(key, 3)
    half_count = OWNERS // 2
    moves = jax.random.randint(key_moves, (half_count,), 0, SEQ_DEV + 1)
    moves = moves.at[0].set(SEQ_DEV)
    order = jax.random.permutation(key_order, OWNERS)
    shifts = jnp.zeros((OWNERS,), jnp.int32).at[order[:half_count]].set(moves).at[order[half_count:]].set(-moves)
    counts = SEQ_DEV + shifts
    ends = jnp.cumsum(counts)
    positions = jnp.arange(EXAMPLES, dtype=jnp.int32)
    assigned = jnp.sum((positions[:, None] >= ends[None, :]).astype(jnp.int32), axis=1)
    shuffle = jax.random.permutation(key_shuffle, EXAMPLES)
    return assigned[shuffle].astype(jnp.int32)


def touch_ends(entries, key, low, largest):
    longest = entries.shape.index(max(entries.shape))
    spots = []
    for shift in (0, 1):
        where = [jax.random.randint(jax.random.fold_in(key, axis), (), 0, length) for axis, length in enumerate(entries.shape)]
        where[longest] = (where[longest] + shift) % entries.shape[longest]
        spots.append(tuple(where))
    return entries.at[spots[0]].set(low).at[spots[1]].set(largest)


def block_levels(rng, extent, pieces, smallest, high):
    level, own = 1.0, jax.random.fold_in(rng, 6)
    for dim, parts in pieces:
        draws = jnp.exp(jax.random.uniform(jax.random.fold_in(own, dim), (parts,), jnp.float32, smallest / len(pieces), high / len(pieces)))
        level = level * jnp.repeat(draws, extent[dim] // parts).reshape([-1 if axis == dim else 1 for axis in range(len(extent))])
    return level


def bell_draw(own_key, shape, width, bound, cuts=(), held_as=jnp.bfloat16):
    factor_of = block_levels(own_key, shape, cuts, -0.22, 0.18) if cuts else 1.0
    result = jax.random.normal(own_key, shape, jnp.float32) * width * factor_of
    return jnp.minimum(jnp.maximum(result, -bound), bound).astype(held_as)


def setup_inputs(seed: int = 0) -> dict:
    streams_of = jax.random.split(jax.random.key(seed), 13)
    return {
        "layer_input": bell_draw(streams_of[0], (TOKENS, D), 1.0, 6.0, ((0, 64), (1, 8))),
        "gate_pre": bell_draw(streams_of[1], (TOKENS, FF), 1.0, 6.0, ((0, 64), (1, 8))),
        "up_pre": bell_draw(streams_of[2], (TOKENS, FF), 1.0, 6.0, ((0, 64), (1, 8))),
        "hidden_grad": bell_draw(streams_of[3], (TOKENS, FF), 1.0, 6.0, ((0, 64), (1, 8))),
        "out_grad": bell_draw(streams_of[4], (TOKENS, D), 1.0, 6.0, ((0, 64), (1, 8))),
        "proj_model_in": bell_draw(streams_of[5], (D, 2 * RANK), D ** -0.5, 0.078125, ((0, 8),)),
        "proj_hidden_in": bell_draw(streams_of[6], (FF, RANK), FF ** -0.5, 0.0546875, ((0, 8),)),
        "proj_hidden_out": bell_draw(streams_of[7], (FF, 2 * RANK), FF ** -0.5, 0.0546875, ((0, 8),)),
        "proj_model_out": bell_draw(streams_of[8], (D, RANK), D ** -0.5, 0.078125, ((0, 8),)),
        "queries": bell_draw(streams_of[9], (NQ, 3, RANK * RANK), (3 * RANK * RANK) ** -0.5, 0.0546875, ((0, 64), (2, 8))),
        "validity": touch_ends((jax.random.randint(streams_of[10], (EXAMPLES, LEN), 0, 4) < 3).astype(jnp.int32), jax.random.fold_in(streams_of[10], 1), 0, 1),
        "owners": draw_owners(jax.random.fold_in(streams_of[12], 71), 0),
    }


def reference(layer_input, gate_pre, up_pre, hidden_grad, out_grad, proj_model_in, proj_hidden_in, proj_hidden_out, proj_model_out, queries, validity, owners):
    scale = LEN ** -0.5

    def one_example(items):
        rows_x, rows_gate, rows_up, rows_dh, rows_dy, weights = items
        gate32 = rows_gate.astype(jnp.float32)
        up32 = rows_up.astype(jnp.float32)
        dh32 = rows_dh.astype(jnp.float32)
        sigma = jax.nn.sigmoid(gate32)
        hidden = (gate32 * sigma * up32).astype(jnp.bfloat16)
        gate_grad = (dh32 * up32 * sigma * (1.0 + gate32 * (1.0 - sigma))).astype(jnp.bfloat16)
        up_grad = (dh32 * (gate32 * sigma)).astype(jnp.bfloat16)
        from_model = jnp.dot(rows_x, proj_model_in, preferred_element_type=jnp.float32)
        in_factors = jnp.stack([from_model[:, :RANK], from_model[:, RANK:], jnp.dot(hidden, proj_hidden_in, preferred_element_type=jnp.float32)], axis=1)
        out_factors = jnp.stack([
            jnp.dot(gate_grad, proj_hidden_out[:, :RANK], preferred_element_type=jnp.float32),
            jnp.dot(up_grad, proj_hidden_out[:, RANK:], preferred_element_type=jnp.float32),
            jnp.dot(rows_dy, proj_model_out, preferred_element_type=jnp.float32)], axis=1)
        summed = jnp.einsum('t,tmi,tmj->mij', weights, out_factors, in_factors, precision=lax.Precision.HIGHEST)
        return (summed * scale).reshape(3, RANK * RANK).astype(jnp.bfloat16)

    sketches = lax.map(one_example, (
        layer_input.reshape(EXAMPLES, LEN, D),
        gate_pre.reshape(EXAMPLES, LEN, FF),
        up_pre.reshape(EXAMPLES, LEN, FF),
        hidden_grad.reshape(EXAMPLES, LEN, FF),
        out_grad.reshape(EXAMPLES, LEN, D),
        validity.astype(jnp.float32)))
    scores = jnp.dot(sketches.reshape(EXAMPLES, 3 * RANK * RANK), queries.reshape(NQ, 3 * RANK * RANK).T, preferred_element_type=jnp.float32)

    def count_step(counts, owner_id):
        slot_id = owner_id * CAP + counts[owner_id]
        counts = counts + (jnp.arange(OWNERS, dtype=jnp.int32) == owner_id).astype(jnp.int32)
        return counts, slot_id

    unused, slot_ids = lax.scan(count_step, jnp.zeros((OWNERS,), jnp.int32), owners.astype(jnp.int32))
    stored = jnp.zeros((OWNERS * CAP, 3, RANK * RANK), jnp.bfloat16).at[slot_ids.astype(jnp.int32)].set(sketches)
    return scores, stored
```

```python
import jax
import jax.numpy as jnp
from jax import lax
from jax.sharding import PartitionSpec as P


def local(
    layer_input,
    gate_pre,
    up_pre,
    hidden_grad,
    out_grad,
    proj_model_in,
    proj_hidden_in,
    proj_hidden_out,
    proj_model_out,
    queries,
    validity,
    owners,
):
    rank = proj_hidden_in.shape[1]
    seq_count, seq_len = validity.shape
    stores = lax.axis_size("store")
    groups = lax.axis_size("fsdp")
    rows = rank // stores
    gate32 = gate_pre.astype(jnp.float32)
    up32 = up_pre.astype(jnp.float32)
    dh32 = hidden_grad.astype(jnp.float32)
    sigma = jax.nn.sigmoid(gate32)
    hidden = (gate32 * sigma * up32).astype(jnp.bfloat16)
    gate_grad = (dh32 * up32 * sigma * (1.0 + gate32 * (1.0 - sigma))).astype(jnp.bfloat16)
    up_grad = (dh32 * (gate32 * sigma)).astype(jnp.bfloat16)

    def factor(proj, act):
        return lax.dot_general(
            proj, act, (((0,), (1,)), ((), ())), preferred_element_type=jnp.float32
        ).astype(jnp.bfloat16)

    tokens = gate_pre.shape[0]
    in_part = jnp.concatenate(
        [factor(proj_model_in, layer_input), factor(proj_hidden_in, hidden)], axis=0
    )
    out_part = jnp.concatenate(
        [
            factor(proj_hidden_out[:, :rank], gate_grad),
            factor(proj_hidden_out[:, rank:], up_grad),
            factor(proj_model_out, out_grad),
        ],
        axis=0,
    )
    out_blocks = out_part.reshape(3, stores, rows, tokens).transpose(1, 0, 2, 3)
    send = jnp.concatenate(
        [
            jnp.broadcast_to(in_part[None], (stores, 3 * rank, tokens)),
            out_blocks.reshape(stores, 3 * rows, tokens),
        ],
        axis=1,
    )
    got = lax.all_to_all(send, "store", 0, 0, tiled=True)
    full = jnp.sum(got.astype(jnp.float32), axis=0)
    in_full = full[: 3 * rank].reshape(3, rank, seq_count, seq_len)
    out_rows = full[3 * rank :].reshape(3, rows, seq_count, seq_len)
    weights = validity.astype(jnp.float32)
    summed = jnp.einsum(
        "mjel,miel->emij",
        in_full,
        out_rows * weights,
        precision=lax.Precision.HIGHEST,
    )
    sketch_local = (summed * float(seq_len) ** (-0.5)).astype(jnp.bfloat16)
    flat_local = sketch_local.reshape(1, seq_count, 3 * rows * rank)
    spread = jnp.broadcast_to(flat_local, (groups, seq_count, 3 * rows * rank))
    gathered = lax.all_to_all(spread, "fsdp", 0, 0, tiled=True)
    flattened = gathered.reshape(groups * seq_count, 3 * rows * rank)
    query_rows = queries.reshape(queries.shape[0], -1)
    partial_scores = lax.dot_general(
        flattened, query_rows, (((1,), (1,)), ((), ())), preferred_element_type=jnp.float32
    )
    capacity = 2 * seq_count
    own_index = lax.axis_index("fsdp")
    is_mine = (owners == own_index).astype(jnp.int32)
    count = owners.shape[0]
    before = lax.broadcasted_iota(jnp.int32, (count, count), 0) < lax.broadcasted_iota(
        jnp.int32, (count, count), 1
    )
    slot_rank = jnp.sum(jnp.where(before, is_mine[:, None], 0), axis=0)
    chooser = (
        (slot_rank[None, :] == jnp.arange(capacity, dtype=jnp.int32)[:, None])
        & (is_mine[None, :] == 1)
    ).astype(jnp.bfloat16)
    kept = jnp.dot(chooser, flattened, preferred_element_type=jnp.float32)
    stored = kept.reshape(capacity, 3, -1).astype(jnp.bfloat16)
    score_blocks = lax.all_to_all(
        partial_scores.reshape(stores, -1, partial_scores.shape[1]), "store", 0, 0, tiled=True
    )
    scores = jnp.sum(score_blocks, axis=0)
    return (scores, stored)


def solution(mesh):
    placed = (
        P("fsdp", "store"),
        P("fsdp", "store"),
        P("fsdp", "store"),
        P("fsdp", "store"),
        P("fsdp", "store"),
        P("store", None),
        P("store", None),
        P("store", None),
        P("store", None),
        P("fsdp", None, "store"),
        P("fsdp", None),
        P(),
    )
    return jax.shard_map(
        local,
        mesh=mesh,
        in_specs=placed,
        out_specs=(P("store", "fsdp"), P("fsdp", None, "store")),
        check_vma=False,
    )
```

```python
import functools

import jax
import jax.numpy as jnp
from jax import lax
from jax.experimental import pallas as pl
from jax.experimental.pallas import tpu as pltpu
from jax.sharding import PartitionSpec as P

BF = jnp.bfloat16
F32 = jnp.float32


def _dot(a, b, ca, cb, **kw):
    return lax.dot_general(
        a, b, (((ca,), (cb,)), ((), ())), preferred_element_type=F32, **kw
    )


def _splits(total, step):
    return [(lo, min(lo + step, total)) for lo in range(0, total, step)]


def factor_kernel(
    stores,
    step,
    x_hbm,
    gate_hbm,
    up_hbm,
    dh_hbm,
    dy_hbm,
    pmi_hbm,
    phi_hbm,
    pho_hbm,
    pmo_hbm,
    out_ref,
    x,
    gate,
    up,
    dh,
    dy,
    pmi,
    phi,
    pho,
    pmo,
    hidden,
    gate_grad,
    up_grad,
    sems,
):
    features, tokens = gate.shape
    rank = phi.shape[0]
    rows = rank // stores
    seq_len = out_ref.shape[2]
    spans = _splits(features, step)
    model = [
        pltpu.make_async_copy(src, dst, sems.at[i])
        for i, (src, dst) in enumerate(
            [(x_hbm, x), (pmi_hbm, pmi), (dy_hbm, dy), (pmo_hbm, pmo), (phi_hbm, phi), (pho_hbm, pho)]
        )
    ]
    parts = [
        [
            pltpu.make_async_copy(
                src.at[pl.ds(lo, hi - lo)], dst.at[pl.ds(lo, hi - lo)], sems.at[6 + 3 * n + i]
            )
            for i, (src, dst) in enumerate([(gate_hbm, gate), (up_hbm, up), (dh_hbm, dh)])
        ]
        for n, (lo, hi) in enumerate(spans)
    ]
    for copy in model + parts[0]:
        copy.start()
    for part in parts[1:]:
        for copy in part:
            copy.start()

    for copy in model[:4]:
        copy.wait()
    from_model = _dot(x[...], pmi[...], 1, 0).T
    out_two = _dot(pmo[...], dy[...], 1, 1)
    for copy in model[4:]:
        copy.wait()
    in_two = out_zero = out_one = None
    for n, (lo, hi) in enumerate(spans):
        for copy in parts[n]:
            copy.wait()
        block = 64

        def body(i, carry, lo=lo):
            at = pl.ds(pl.multiple_of(lo + i * block, block), block)
            g = gate[at].astype(F32)
            u = up[at].astype(F32)
            d = dh[at].astype(F32)
            sigma = 0.5 * jnp.tanh(0.5 * g) + 0.5
            silu = g * sigma
            hidden[at] = (silu * u).astype(BF)
            up_grad[at] = (d * silu).astype(BF)
            gate_grad[at] = (d * u * (sigma + silu * (1.0 - sigma))).astype(BF)
            return carry

        lax.fori_loop(0, (hi - lo) // block, body, 0, unroll=True)
        a = _dot(phi[:, lo:hi], hidden[lo:hi], 1, 0)
        b = _dot(pho[lo:hi, :rank], gate_grad[lo:hi], 0, 0)
        c = _dot(pho[lo:hi, rank:], up_grad[lo:hi], 0, 0)
        in_two = a if in_two is None else in_two + a
        out_zero = b if out_zero is None else out_zero + b
        out_one = c if out_one is None else out_one + c

    out_all = [out_zero, out_one, out_two]
    for e in range(2):
        at = slice(e * seq_len, (e + 1) * seq_len)
        factors = jnp.concatenate([from_model[:, at], in_two[:, at]], axis=0).astype(BF)
        for s in range(e, stores, 2):
            out_ref[s, : 3 * rank] = factors
            for m in range(3):
                mine = out_all[m][s * rows : (s + 1) * rows, at]
                other = out_all[m][(s ^ 1) * rows : ((s ^ 1) + 1) * rows, at]
                lo = 3 * rank + m * 2 * rows
                out_ref[s, lo : lo + 2 * rows] = jnp.concatenate([mine, other], axis=0).astype(BF)


def sketch_kernel(scale, got, weights, out_ref, total):
    stores = got.shape[0]
    acc = got[0].astype(F32)
    for s in range(1, stores):
        acc = acc + got[s].astype(F32)
    total[...] = acc
    rank = 64
    blocks = []
    for m in range(3):
        lo = 3 * rank + m * 16
        factor = total[m * rank : (m + 1) * rank]
        halves = []
        for parity in range(2):
            picked = total[pl.ds(lo + parity, 8, stride=2)] * weights[...]
            halves.append(_dot(picked, factor, 1, 1, precision=lax.Precision.HIGHEST))
        blocks.append(jnp.concatenate(halves, axis=1))
    sketch = (jnp.concatenate(blocks, axis=0) * scale).astype(BF)

    def body(i, carry):
        out_ref[i] = sketch
        return carry

    lax.fori_loop(0, out_ref.shape[0], body, 0, unroll=8)


def score_kernel(gathered, mine, other, scores, wide):
    groups, lines, lanes = gathered.shape
    wide[...] = gathered[...].astype(F32).reshape(groups * lines, lanes)
    acc = None
    for m in range(3):
        for h, query in enumerate((mine, other)):
            cols = [wide[pl.ds(m * 8 + h * 4 + p, groups, stride=lines)] for p in range(4)]
            block = jnp.concatenate(cols, axis=1).astype(BF)
            term = _dot(block, query[m], 1, 1)
            acc = term if acc is None else acc + term
    scores[...] = acc


def keep_kernel(chosen, valid, gathered, after, kept):
    for slot in range(kept.shape[0]):
        picked = gathered[chosen[slot]].astype(F32)
        kept[slot] = jnp.where(valid[slot] == 1, picked, 0.0).astype(BF)


def finish_kernel(parts, own, received, scores, stored):
    chips = parts.shape[0] // 2
    per_core = []
    for core in range(2):
        total = parts[core]
        for chip in range(1, chips):
            total = total + parts[2 * chip + core]
        per_core.append(total)
    for z in range(per_core[0].shape[0]):
        for core in range(2):
            scores[2 * z + core : 2 * z + core + 1] = per_core[core][z : z + 1]
    for m in range(3):
        stored[m] = (own[m].astype(F32) + received[m].astype(F32)).astype(BF)


def _vmem(n):
    return [pl.BlockSpec(memory_space=pltpu.VMEM)] * n


def local(
    layer_input,
    gate_pre,
    up_pre,
    hidden_grad,
    out_grad,
    proj_model_in,
    proj_hidden_in,
    proj_hidden_out,
    proj_model_out,
    queries,
    validity,
    owners,
):
    tokens, features = gate_pre.shape
    width = layer_input.shape[1]
    rank = proj_hidden_in.shape[1]
    seq_count, seq_len = validity.shape
    stores = lax.axis_size("store")
    groups = lax.axis_size("fsdp")
    rows = rank // stores
    capacity = 2 * seq_count
    core = lax.axis_index("store") % 2

    step = 512
    spans = len(_splits(features, step))
    lines = 3 * rank + 3 * 2 * rows
    send = pl.pallas_call(
        functools.partial(factor_kernel, stores, step),
        out_shape=jax.ShapeDtypeStruct((stores, lines, seq_len), BF),
        in_specs=[pl.BlockSpec(memory_space=pl.ANY)] * 9,
        out_specs=pl.BlockSpec(memory_space=pltpu.VMEM),
        scratch_shapes=[
            pltpu.VMEM((tokens, width), BF),
            pltpu.VMEM((features, tokens), BF),
            pltpu.VMEM((features, tokens), BF),
            pltpu.VMEM((features, tokens), BF),
            pltpu.VMEM((tokens, width), BF),
            pltpu.VMEM((width, 2 * rank), BF),
            pltpu.VMEM((rank, features), BF),
            pltpu.VMEM((features, 2 * rank), BF),
            pltpu.VMEM((rank, width), BF),
            pltpu.VMEM((features, tokens), BF),
            pltpu.VMEM((features, tokens), BF),
            pltpu.VMEM((features, tokens), BF),
            pltpu.SemaphoreType.DMA((6 + 3 * spans,)),
        ],
        compiler_params=pltpu.CompilerParams(vmem_limit_bytes=60 * 2**20),
        name="factors",
    )(
        layer_input,
        gate_pre.T,
        up_pre.T,
        hidden_grad.T,
        out_grad,
        proj_model_in,
        proj_hidden_in.T,
        proj_hidden_out,
        proj_model_out.T,
    )
    got = lax.all_to_all(send, "store", 0, 0, tiled=True)

    weights = jnp.where(core == 0, validity[0], validity[1]).astype(F32).reshape(1, seq_len)
    lines = 3 * 2 * rows * rank // 128
    spread = pl.pallas_call(
        functools.partial(sketch_kernel, float(seq_len) ** (-0.5)),
        out_shape=jax.ShapeDtypeStruct((groups, lines, 128), BF),
        in_specs=_vmem(2),
        out_specs=pl.BlockSpec(memory_space=pltpu.VMEM),
        scratch_shapes=[pltpu.VMEM(got.shape[1:], F32)],
        compiler_params=pltpu.CompilerParams(vmem_limit_bytes=8 * 2**20),
        name="sketch",
    )(got, weights)
    flip = [(s, s ^ 1) for s in range(stores)]
    query_rows = queries.transpose(1, 0, 2)
    other_rows = lax.ppermute(query_rows, "store", flip)
    gathered = lax.all_to_all(spread, "fsdp", 0, 0, tiled=True)

    own_index = lax.axis_index("fsdp")
    mine = (owners == own_index).astype(jnp.int32)
    count = owners.shape[0]
    first = lax.broadcasted_iota(jnp.int32, (count, count), 0)
    second = lax.broadcasted_iota(jnp.int32, (count, count), 1)
    slot_rank = jnp.sum(jnp.where(first < second, mine[:, None], 0), axis=0)
    slots = jnp.arange(capacity, dtype=jnp.int32)
    sequence = jnp.arange(count, dtype=jnp.int32)
    hit = (
        (slot_rank[None, :] == slots[:, None])
        & (mine[None, :] == 1)
        & (sequence[None, :] % seq_count == core)
    ).astype(jnp.int32)
    valid = jnp.sum(hit, axis=1)
    chosen = jnp.clip(jnp.sum(hit * (sequence // seq_count)[None, :], axis=1), 0, groups - 1)

    query_count = queries.shape[0]
    partial_scores = pl.pallas_call(
        score_kernel,
        out_shape=jax.ShapeDtypeStruct((groups, query_count), F32),
        in_specs=_vmem(3),
        out_specs=pl.BlockSpec(memory_space=pltpu.VMEM),
        scratch_shapes=[pltpu.VMEM((groups * lines, 128), F32)],
        compiler_params=pltpu.CompilerParams(vmem_limit_bytes=12 * 2**20),
        name="scores",
    )(gathered, query_rows, other_rows)
    kept = pl.pallas_call(
        keep_kernel,
        out_shape=jax.ShapeDtypeStruct((capacity, lines, 128), BF),
        in_specs=[pl.BlockSpec(memory_space=pltpu.SMEM)] * 2
        + _vmem(1)
        + [pl.BlockSpec(memory_space=pl.ANY)],
        out_specs=pl.BlockSpec(memory_space=pltpu.VMEM),
        cost_estimate=pl.CostEstimate(flops=0, bytes_accessed=8 * 2**20, transcendentals=0),
        compiler_params=pltpu.CompilerParams(vmem_limit_bytes=8 * 2**20),
        name="kept",
    )(chosen, valid, gathered, partial_scores)

    parts = lax.all_to_all(
        partial_scores.reshape(stores, groups // stores, query_count), "store", 0, 0, tiled=True
    )
    kept = kept.reshape(capacity, 3, 2, -1).transpose(2, 1, 0, 3)
    received = lax.ppermute(kept[1], "store", flip)
    scores, stored = pl.pallas_call(
        finish_kernel,
        out_shape=(
            jax.ShapeDtypeStruct((2 * groups // stores, query_count), F32),
            jax.ShapeDtypeStruct(kept.shape[1:], BF),
        ),
        in_specs=_vmem(3),
        out_specs=tuple(_vmem(2)),
        compiler_params=pltpu.CompilerParams(vmem_limit_bytes=8 * 2**20),
        name="finish",
    )(parts, kept[0], received)
    stored = stored.transpose(1, 0, 2)
    return (scores, stored)


def solution(mesh):
    placed = (
        P("fsdp", "store"),
        P("fsdp", "store"),
        P("fsdp", "store"),
        P("fsdp", "store"),
        P("fsdp", "store"),
        P("store", None),
        P("store", None),
        P("store", None),
        P("store", None),
        P("fsdp", None, "store"),
        P("fsdp", None),
        P(),
    )
    return jax.shard_map(
        local,
        mesh=mesh,
        in_specs=placed,
        out_specs=(P("store", "fsdp"), P("fsdp", None, "store")),
        check_vma=False,
    )
```

```python
import functools

import jax
import jax.numpy as jnp
import numpy as np
from jax import lax
from jax.experimental import pallas as pl
from jax.experimental.pallas import tpu as pltpu
from jax.sharding import PartitionSpec as P

BF = jnp.bfloat16
F32 = jnp.float32
GROUP_SEED = 2
STORE_SEED = 5


def _order(count, seed):
    if seed is None:
        return list(range(count))
    return [int(i) for i in np.random.RandomState(seed).permutation(count)]


def _exchange(x, axis, order):
    plain = order == sorted(order)
    groups = None if plain else [order]
    return lax.all_to_all(x, axis, 0, 0, tiled=True, axis_index_groups=groups)


def _dot(a, b, ca, cb, **kw):
    return lax.dot_general(
        a, b, (((ca,), (cb,)), ((), ())), preferred_element_type=F32, **kw
    )


def _splits(total, step):
    return [(lo, min(lo + step, total)) for lo in range(0, total, step)]


def factor_kernel(
    stores,
    step,
    store_order,
    x_hbm,
    gate_hbm,
    up_hbm,
    dh_hbm,
    dy_hbm,
    pmi_hbm,
    phi_hbm,
    pho_hbm,
    pmo_hbm,
    out_ref,
    x,
    gate,
    up,
    dh,
    dy,
    pmi,
    phi,
    pho,
    pmo,
    hidden,
    gate_grad,
    up_grad,
    sems,
):
    features, tokens = gate.shape
    rank = phi.shape[0]
    rows = rank // stores
    seq_len = out_ref.shape[2]
    spans = _splits(features, step)
    model = [
        pltpu.make_async_copy(src, dst, sems.at[i])
        for i, (src, dst) in enumerate(
            [(x_hbm, x), (pmi_hbm, pmi), (dy_hbm, dy), (pmo_hbm, pmo), (phi_hbm, phi), (pho_hbm, pho)]
        )
    ]
    parts = [
        [
            pltpu.make_async_copy(
                src.at[pl.ds(lo, hi - lo)], dst.at[pl.ds(lo, hi - lo)], sems.at[6 + 3 * n + i]
            )
            for i, (src, dst) in enumerate([(gate_hbm, gate), (up_hbm, up), (dh_hbm, dh)])
        ]
        for n, (lo, hi) in enumerate(spans)
    ]
    for copy in model + parts[0]:
        copy.start()
    for part in parts[1:]:
        for copy in part:
            copy.start()

    for copy in model[:4]:
        copy.wait()
    from_model = _dot(x[...], pmi[...], 1, 0).T
    out_two = _dot(pmo[...], dy[...], 1, 1)
    for copy in model[4:]:
        copy.wait()
    in_two = out_zero = out_one = None
    for n, (lo, hi) in enumerate(spans):
        for copy in parts[n]:
            copy.wait()
        block = 64

        def body(i, carry, lo=lo):
            at = pl.ds(pl.multiple_of(lo + i * block, block), block)
            g = gate[at].astype(F32)
            u = up[at].astype(F32)
            d = dh[at].astype(F32)
            sigma = 0.5 * jnp.tanh(0.5 * g) + 0.5
            silu = g * sigma
            hidden[at] = (silu * u).astype(BF)
            up_grad[at] = (d * silu).astype(BF)
            gate_grad[at] = (d * u * (sigma + silu * (1.0 - sigma))).astype(BF)
            return carry

        lax.fori_loop(0, (hi - lo) // block, body, 0, unroll=True)
        a = _dot(phi[:, lo:hi], hidden[lo:hi], 1, 0)
        b = _dot(pho[lo:hi, :rank], gate_grad[lo:hi], 0, 0)
        c = _dot(pho[lo:hi, rank:], up_grad[lo:hi], 0, 0)
        in_two = a if in_two is None else in_two + a
        out_zero = b if out_zero is None else out_zero + b
        out_one = c if out_one is None else out_one + c

    out_all = [out_zero, out_one, out_two]
    for e in range(2):
        at = slice(e * seq_len, (e + 1) * seq_len)
        factors = jnp.concatenate([from_model[:, at], in_two[:, at]], axis=0).astype(BF)
        for s in range(e, stores, 2):
            place = store_order.index(s)
            out_ref[place, : 3 * rank] = factors
            for m in range(3):
                mine = out_all[m][s * rows : (s + 1) * rows, at]
                other = out_all[m][(s ^ 1) * rows : ((s ^ 1) + 1) * rows, at]
                lo = 3 * rank + m * 2 * rows
                out_ref[place, lo : lo + 2 * rows] = jnp.concatenate([mine, other], axis=0).astype(BF)


def sketch_kernel(scale, got, weights, out_ref, total):
    stores = got.shape[0]
    acc = got[0].astype(F32)
    for s in range(1, stores):
        acc = acc + got[s].astype(F32)
    total[...] = acc
    rank = 64
    blocks = []
    for m in range(3):
        lo = 3 * rank + m * 16
        factor = total[m * rank : (m + 1) * rank]
        halves = []
        for parity in range(2):
            picked = total[pl.ds(lo + parity, 8, stride=2)] * weights[...]
            halves.append(_dot(picked, factor, 1, 1, precision=lax.Precision.HIGHEST))
        blocks.append(jnp.concatenate(halves, axis=1))
    sketch = (jnp.concatenate(blocks, axis=0) * scale).astype(BF)

    def body(i, carry):
        out_ref[i] = sketch
        return carry

    lax.fori_loop(0, out_ref.shape[0], body, 0, unroll=8)


def score_kernel(places, gathered, mine, other, scores, wide):
    groups, lines, lanes = gathered.shape
    for i, place in enumerate(places):
        wide[place * lines : (place + 1) * lines] = gathered[i].astype(F32)
    acc = None
    for m in range(3):
        for h, query in enumerate((mine, other)):
            cols = [wide[pl.ds(m * 8 + h * 4 + p, groups, stride=lines)] for p in range(4)]
            block = jnp.concatenate(cols, axis=1).astype(BF)
            term = _dot(block, query[m], 1, 1)
            acc = term if acc is None else acc + term
    scores[...] = acc


def keep_kernel(chosen, valid, gathered, after, kept):
    for slot in range(kept.shape[0]):
        picked = gathered[chosen[slot]].astype(F32)
        kept[slot] = jnp.where(valid[slot] == 1, picked, 0.0).astype(BF)


def finish_kernel(store_order, parts, own, received, scores, stored):
    per_core = []
    for core in range(2):
        first, *others = [i for i, s in enumerate(store_order) if s % 2 == core]
        total = parts[first]
        for i in others:
            total = total + parts[i]
        per_core.append(total)
    for z in range(per_core[0].shape[0]):
        for core in range(2):
            scores[2 * z + core : 2 * z + core + 1] = per_core[core][z : z + 1]
    for m in range(3):
        stored[m] = (own[m].astype(F32) + received[m].astype(F32)).astype(BF)


def _vmem(n):
    return [pl.BlockSpec(memory_space=pltpu.VMEM)] * n


def local(
    layer_input,
    gate_pre,
    up_pre,
    hidden_grad,
    out_grad,
    proj_model_in,
    proj_hidden_in,
    proj_hidden_out,
    proj_model_out,
    queries,
    validity,
    owners,
):
    tokens, features = gate_pre.shape
    width = layer_input.shape[1]
    rank = proj_hidden_in.shape[1]
    seq_count, seq_len = validity.shape
    stores = lax.axis_size("store")
    groups = lax.axis_size("fsdp")
    rows = rank // stores
    capacity = 2 * seq_count
    core = lax.axis_index("store") % 2
    store_order = _order(stores, STORE_SEED)
    group_order = _order(groups, GROUP_SEED)

    step = 512
    spans = len(_splits(features, step))
    lines = 3 * rank + 3 * 2 * rows
    send = pl.pallas_call(
        functools.partial(factor_kernel, stores, step, store_order),
        out_shape=jax.ShapeDtypeStruct((stores, lines, seq_len), BF),
        in_specs=[pl.BlockSpec(memory_space=pl.ANY)] * 9,
        out_specs=pl.BlockSpec(memory_space=pltpu.VMEM),
        scratch_shapes=[
            pltpu.VMEM((tokens, width), BF),
            pltpu.VMEM((features, tokens), BF),
            pltpu.VMEM((features, tokens), BF),
            pltpu.VMEM((features, tokens), BF),
            pltpu.VMEM((tokens, width), BF),
            pltpu.VMEM((width, 2 * rank), BF),
            pltpu.VMEM((rank, features), BF),
            pltpu.VMEM((features, 2 * rank), BF),
            pltpu.VMEM((rank, width), BF),
            pltpu.VMEM((features, tokens), BF),
            pltpu.VMEM((features, tokens), BF),
            pltpu.VMEM((features, tokens), BF),
            pltpu.SemaphoreType.DMA((6 + 3 * spans,)),
        ],
        compiler_params=pltpu.CompilerParams(vmem_limit_bytes=60 * 2**20),
        name="factors",
    )(
        layer_input,
        gate_pre.T,
        up_pre.T,
        hidden_grad.T,
        out_grad,
        proj_model_in,
        proj_hidden_in.T,
        proj_hidden_out,
        proj_model_out.T,
    )
    got = _exchange(send, "store", store_order)

    weights = jnp.where(core == 0, validity[0], validity[1]).astype(F32).reshape(1, seq_len)
    lines = 3 * 2 * rows * rank // 128
    spread = pl.pallas_call(
        functools.partial(sketch_kernel, float(seq_len) ** (-0.5)),
        out_shape=jax.ShapeDtypeStruct((groups, lines, 128), BF),
        in_specs=_vmem(2),
        out_specs=pl.BlockSpec(memory_space=pltpu.VMEM),
        scratch_shapes=[pltpu.VMEM(got.shape[1:], F32)],
        compiler_params=pltpu.CompilerParams(vmem_limit_bytes=8 * 2**20),
        name="sketch",
    )(got, weights)
    flip = [(s, s ^ 1) for s in range(stores)]
    query_rows = queries.transpose(1, 0, 2)
    other_rows = lax.ppermute(query_rows, "store", flip)
    gathered = _exchange(spread, "fsdp", group_order)

    own_index = lax.axis_index("fsdp")
    mine = (owners == own_index).astype(jnp.int32)
    count = owners.shape[0]
    first = lax.broadcasted_iota(jnp.int32, (count, count), 0)
    second = lax.broadcasted_iota(jnp.int32, (count, count), 1)
    slot_rank = jnp.sum(jnp.where(first < second, mine[:, None], 0), axis=0)
    slots = jnp.arange(capacity, dtype=jnp.int32)
    arrival = np.argsort(group_order).astype(np.int32)
    sequence = np.arange(count, dtype=np.int32)
    hit = (
        (slot_rank[None, :] == slots[:, None])
        & (mine[None, :] == 1)
        & (sequence[None, :] % seq_count == core)
    ).astype(jnp.int32)
    valid = jnp.sum(hit, axis=1)
    chosen = jnp.clip(jnp.sum(hit * arrival[sequence // seq_count][None, :], axis=1), 0, groups - 1)

    query_count = queries.shape[0]
    share = groups // stores
    places = [store_order.index(g // share) * share + g % share for g in group_order]
    partial_scores = pl.pallas_call(
        functools.partial(score_kernel, places),
        out_shape=jax.ShapeDtypeStruct((groups, query_count), F32),
        in_specs=_vmem(3),
        out_specs=pl.BlockSpec(memory_space=pltpu.VMEM),
        scratch_shapes=[pltpu.VMEM((groups * lines, 128), F32)],
        compiler_params=pltpu.CompilerParams(vmem_limit_bytes=12 * 2**20),
        name="scores",
    )(gathered, query_rows, other_rows)
    kept = pl.pallas_call(
        keep_kernel,
        out_shape=jax.ShapeDtypeStruct((capacity, lines, 128), BF),
        in_specs=[pl.BlockSpec(memory_space=pltpu.SMEM)] * 2
        + _vmem(1)
        + [pl.BlockSpec(memory_space=pl.ANY)],
        out_specs=pl.BlockSpec(memory_space=pltpu.VMEM),
        cost_estimate=pl.CostEstimate(flops=0, bytes_accessed=8 * 2**20, transcendentals=0),
        compiler_params=pltpu.CompilerParams(vmem_limit_bytes=8 * 2**20),
        name="kept",
    )(chosen, valid, gathered, partial_scores)

    parts = _exchange(
        partial_scores.reshape(stores, share, query_count), "store", store_order
    )
    kept = kept.reshape(capacity, 3, 2, -1).transpose(2, 1, 0, 3)
    received = lax.ppermute(kept[1], "store", flip)
    scores, stored = pl.pallas_call(
        functools.partial(finish_kernel, store_order),
        out_shape=(
            jax.ShapeDtypeStruct((2 * groups // stores, query_count), F32),
            jax.ShapeDtypeStruct(kept.shape[1:], BF),
        ),
        in_specs=_vmem(3),
        out_specs=tuple(_vmem(2)),
        compiler_params=pltpu.CompilerParams(vmem_limit_bytes=8 * 2**20),
        name="finish",
    )(parts, kept[0], received)
    stored = stored.transpose(1, 0, 2)
    return (scores, stored)


def solution(mesh):
    placed = (
        P("fsdp", "store"),
        P("fsdp", "store"),
        P("fsdp", "store"),
        P("fsdp", "store"),
        P("fsdp", "store"),
        P("store", None),
        P("store", None),
        P("store", None),
        P("store", None),
        P("fsdp", None, "store"),
        P("fsdp", None),
        P(),
    )
    return jax.shard_map(
        local,
        mesh=mesh,
        in_specs=placed,
        out_specs=(P("store", "fsdp"), P("fsdp", None, "store")),
        check_vma=False,
    )
```

```python
import functools

import jax
import jax.numpy as jnp
import numpy as np
from jax import lax
from jax.experimental import pallas as pl
from jax.experimental.pallas import tpu as pltpu
from jax.sharding import PartitionSpec as P

BF = jnp.bfloat16
F32 = jnp.float32
GROUP_SEED = 2
STORE_SEED = 8


def _order(count, seed):
    if seed is None:
        return list(range(count))
    return [int(i) for i in np.random.RandomState(seed).permutation(count)]


def _exchange(x, axis, order):
    plain = order == sorted(order)
    groups = None if plain else [order]
    return lax.all_to_all(x, axis, 0, 0, tiled=True, axis_index_groups=groups)


def _dot(a, b, ca, cb, **kw):
    return lax.dot_general(
        a, b, (((ca,), (cb,)), ((), ())), preferred_element_type=F32, **kw
    )


def _splits(total, step):
    return [(lo, min(lo + step, total)) for lo in range(0, total, step)]


def factor_kernel(
    stores,
    step,
    store_order,
    x_hbm,
    gate_hbm,
    up_hbm,
    dh_hbm,
    dy_hbm,
    pmi_hbm,
    phi_hbm,
    pho_hbm,
    pmo_hbm,
    out_ref,
    x,
    gate,
    up,
    dh,
    dy,
    pmi,
    phi,
    pho,
    pmo,
    hidden,
    gate_grad,
    up_grad,
    sems,
):
    features, tokens = gate.shape
    rank = phi.shape[0]
    rows = rank // stores
    seq_len = out_ref.shape[2]
    spans = _splits(features, step)
    model = [
        pltpu.make_async_copy(src, dst, sems.at[i])
        for i, (src, dst) in enumerate(
            [(x_hbm, x), (pmi_hbm, pmi), (dy_hbm, dy), (pmo_hbm, pmo), (phi_hbm, phi), (pho_hbm, pho)]
        )
    ]
    parts = [
        [
            pltpu.make_async_copy(
                src.at[pl.ds(lo, hi - lo)], dst.at[pl.ds(lo, hi - lo)], sems.at[6 + 3 * n + i]
            )
            for i, (src, dst) in enumerate([(gate_hbm, gate), (up_hbm, up), (dh_hbm, dh)])
        ]
        for n, (lo, hi) in enumerate(spans)
    ]
    for copy in model + parts[0]:
        copy.start()
    for part in parts[1:]:
        for copy in part:
            copy.start()

    for copy in model[:4]:
        copy.wait()
    from_model = _dot(x[...], pmi[...], 1, 0).T
    out_two = _dot(pmo[...], dy[...], 1, 1)
    for copy in model[4:]:
        copy.wait()
    in_two = out_zero = out_one = None
    for n, (lo, hi) in enumerate(spans):
        for copy in parts[n]:
            copy.wait()
        block = 64

        def body(i, carry, lo=lo):
            at = pl.ds(pl.multiple_of(lo + i * block, block), block)
            g = gate[at].astype(F32)
            u = up[at].astype(F32)
            d = dh[at].astype(F32)
            sigma = 0.5 * jnp.tanh(0.5 * g) + 0.5
            silu = g * sigma
            hidden[at] = (silu * u).astype(BF)
            up_grad[at] = (d * silu).astype(BF)
            gate_grad[at] = (d * u * (sigma + silu * (1.0 - sigma))).astype(BF)
            return carry

        lax.fori_loop(0, (hi - lo) // block, body, 0, unroll=True)
        a = _dot(phi[:, lo:hi], hidden[lo:hi], 1, 0)
        b = _dot(pho[lo:hi, :rank], gate_grad[lo:hi], 0, 0)
        c = _dot(pho[lo:hi, rank:], up_grad[lo:hi], 0, 0)
        in_two = a if in_two is None else in_two + a
        out_zero = b if out_zero is None else out_zero + b
        out_one = c if out_one is None else out_one + c

    out_all = [out_zero, out_one, out_two]
    for e in range(2):
        at = slice(e * seq_len, (e + 1) * seq_len)
        factors = jnp.concatenate([from_model[:, at], in_two[:, at]], axis=0).astype(BF)
        for s in range(e, stores, 2):
            place = store_order.index(s)
            out_ref[place, : 3 * rank] = factors
            for m in range(3):
                mine = out_all[m][s * rows : (s + 1) * rows, at]
                other = out_all[m][(s ^ 1) * rows : ((s ^ 1) + 1) * rows, at]
                lo = 3 * rank + m * 2 * rows
                out_ref[place, lo : lo + 2 * rows] = jnp.concatenate([mine, other], axis=0).astype(BF)


def sketch_kernel(scale, got, weights, chooser, out_ref, total):
    stores = got.shape[0]
    acc = got[0].astype(F32)
    for s in range(1, stores):
        acc = acc + got[s].astype(F32)
    total[...] = acc
    rank = 64
    blocks = []
    for m in range(3):
        lo = 3 * rank + m * 16
        factor = total[m * rank : (m + 1) * rank]
        picked = [total[pl.ds(lo + parity, 8, stride=2)] for parity in range(2)]
        picked = jnp.concatenate(picked, axis=0) * weights[...]
        both = _dot(picked, factor, 1, 1, precision=lax.Precision.HIGHEST)
        blocks.append(jnp.concatenate([both[:8], both[8:]], axis=1))
    sketch = (jnp.concatenate(blocks, axis=0) * scale).astype(BF)

    def body(i, carry):
        out_ref[i] = sketch
        return carry

    lax.fori_loop(0, out_ref.shape[0], body, 0, unroll=8)


def score_kernel(places, gathered, mine, other, chooser, scores, kept, passed, wide):
    groups, lines, lanes = gathered.shape
    capacity = kept.shape[1]
    for i, place in enumerate(places):
        wide[place * lines : (place + 1) * lines] = gathered[i].astype(F32)
    acc = None
    for m in range(3):
        for h, (query, held) in enumerate(((mine, kept), (other, passed))):
            cols = [wide[pl.ds(m * 8 + h * 4 + p, groups, stride=lines)] for p in range(4)]
            block = jnp.concatenate(cols, axis=1).astype(BF)
            term = _dot(block, query[m], 1, 1)
            acc = term if acc is None else acc + term
            held[m] = _dot(chooser[...], block, 1, 0)[:capacity].astype(BF)
    scores[...] = acc


def finish_kernel(store_order, parts, own, received, scores, stored):
    per_core = []
    for core in range(2):
        first, *others = [i for i, s in enumerate(store_order) if s % 2 == core]
        total = parts[first]
        for i in others:
            total = total + parts[i]
        per_core.append(total)
    for z in range(per_core[0].shape[0]):
        for core in range(2):
            scores[2 * z + core : 2 * z + core + 1] = per_core[core][z : z + 1]
    for m in range(3):
        stored[m] = (own[m].astype(F32) + received[m].astype(F32)).astype(BF)


def _vmem(n):
    return [pl.BlockSpec(memory_space=pltpu.VMEM)] * n


def local(
    layer_input,
    gate_pre,
    up_pre,
    hidden_grad,
    out_grad,
    proj_model_in,
    proj_hidden_in,
    proj_hidden_out,
    proj_model_out,
    queries,
    validity,
    owners,
):
    tokens, features = gate_pre.shape
    width = layer_input.shape[1]
    rank = proj_hidden_in.shape[1]
    seq_count, seq_len = validity.shape
    stores = lax.axis_size("store")
    groups = lax.axis_size("fsdp")
    rows = rank // stores
    capacity = 2 * seq_count
    core = lax.axis_index("store") % 2
    store_order = _order(stores, STORE_SEED)
    group_order = _order(groups, GROUP_SEED)

    step = 512
    spans = len(_splits(features, step))
    lines = 3 * rank + 3 * 2 * rows
    send = pl.pallas_call(
        functools.partial(factor_kernel, stores, step, store_order),
        out_shape=jax.ShapeDtypeStruct((stores, lines, seq_len), BF),
        in_specs=[pl.BlockSpec(memory_space=pl.ANY)] * 9,
        out_specs=pl.BlockSpec(memory_space=pltpu.VMEM),
        scratch_shapes=[
            pltpu.VMEM((tokens, width), BF),
            pltpu.VMEM((features, tokens), BF),
            pltpu.VMEM((features, tokens), BF),
            pltpu.VMEM((features, tokens), BF),
            pltpu.VMEM((tokens, width), BF),
            pltpu.VMEM((width, 2 * rank), BF),
            pltpu.VMEM((rank, features), BF),
            pltpu.VMEM((features, 2 * rank), BF),
            pltpu.VMEM((rank, width), BF),
            pltpu.VMEM((features, tokens), BF),
            pltpu.VMEM((features, tokens), BF),
            pltpu.VMEM((features, tokens), BF),
            pltpu.SemaphoreType.DMA((6 + 3 * spans,)),
        ],
        compiler_params=pltpu.CompilerParams(vmem_limit_bytes=60 * 2**20),
        name="factors",
    )(
        layer_input,
        gate_pre.T,
        up_pre.T,
        hidden_grad.T,
        out_grad,
        proj_model_in,
        proj_hidden_in.T,
        proj_hidden_out,
        proj_model_out.T,
    )
    got = _exchange(send, "store", store_order)

    share = groups // stores
    places = [store_order.index(g // share) * share + g % share for g in group_order]
    at_place = np.argsort([store_order.index(g // share) * share + g % share for g in range(groups)])
    own_index = lax.axis_index("fsdp")
    mine = (owners == own_index).astype(jnp.int32)
    count = owners.shape[0]
    first = lax.broadcasted_iota(jnp.int32, (count, count), 0)
    second = lax.broadcasted_iota(jnp.int32, (count, count), 1)
    slot_rank = jnp.sum(jnp.where(first < second, mine[:, None], 0), axis=0)
    slots = jnp.arange(8, dtype=jnp.int32)
    hit = ((slot_rank[None, :] == slots[:, None]) & (mine[None, :] == 1)).astype(BF)
    wanted = jnp.asarray(seq_count * at_place.astype(np.int32)) + core
    chooser = jnp.dot(
        hit,
        (jnp.arange(count, dtype=jnp.int32)[:, None] == wanted[None, :]).astype(BF),
        preferred_element_type=F32,
    ).astype(BF)

    weights = jnp.where(core == 0, validity[0], validity[1]).astype(F32).reshape(1, seq_len)
    lines = 3 * 2 * rows * rank // 128
    spread = pl.pallas_call(
        functools.partial(sketch_kernel, float(seq_len) ** (-0.5)),
        out_shape=jax.ShapeDtypeStruct((groups, lines, 128), BF),
        in_specs=_vmem(2) + [pl.BlockSpec(memory_space=pl.ANY)],
        out_specs=pl.BlockSpec(memory_space=pltpu.VMEM),
        scratch_shapes=[pltpu.VMEM(got.shape[1:], F32)],
        compiler_params=pltpu.CompilerParams(vmem_limit_bytes=8 * 2**20),
        name="sketch",
    )(got, weights, chooser)
    flip = [(s, s ^ 1) for s in range(stores)]
    query_rows = queries.transpose(1, 0, 2)
    other_rows = lax.ppermute(query_rows, "store", flip)
    gathered = _exchange(spread, "fsdp", group_order)

    query_count = queries.shape[0]
    held = jax.ShapeDtypeStruct((3, capacity, rows * rank), BF)
    partial_scores, kept, passed = pl.pallas_call(
        functools.partial(score_kernel, places),
        out_shape=(jax.ShapeDtypeStruct((groups, query_count), F32), held, held),
        in_specs=_vmem(4),
        out_specs=tuple(_vmem(3)),
        scratch_shapes=[pltpu.VMEM((groups * lines, 128), F32)],
        compiler_params=pltpu.CompilerParams(vmem_limit_bytes=12 * 2**20),
        name="scores",
    )(gathered, query_rows, other_rows, chooser)

    parts = _exchange(
        partial_scores.reshape(stores, share, query_count), "store", store_order
    )
    received = lax.ppermute(passed, "store", flip)
    scores, stored = pl.pallas_call(
        functools.partial(finish_kernel, store_order),
        out_shape=(
            jax.ShapeDtypeStruct((2 * groups // stores, query_count), F32),
            held,
        ),
        in_specs=_vmem(3),
        out_specs=tuple(_vmem(2)),
        compiler_params=pltpu.CompilerParams(vmem_limit_bytes=8 * 2**20),
        name="finish",
    )(parts, kept, received)
    stored = stored.transpose(1, 0, 2)
    return (scores, stored)


def solution(mesh):
    placed = (
        P("fsdp", "store"),
        P("fsdp", "store"),
        P("fsdp", "store"),
        P("fsdp", "store"),
        P("fsdp", "store"),
        P("store", None),
        P("store", None),
        P("store", None),
        P("store", None),
        P("fsdp", None, "store"),
        P("fsdp", None),
        P(),
    )
    return jax.shard_map(
        local,
        mesh=mesh,
        in_specs=placed,
        out_specs=(P("store", "fsdp"), P("fsdp", None, "store")),
        check_vma=False,
    )
```

```python
import functools

import jax
import jax.numpy as jnp
import numpy as np
from jax import lax
from jax.experimental import pallas as pl
from jax.experimental.pallas import tpu as pltpu
from jax.sharding import PartitionSpec as P

BF = jnp.bfloat16
F32 = jnp.float32
GROUP_SEED = 2
STORE_SEED = 8


def _order(count, seed):
    if seed is None:
        return list(range(count))
    return [int(i) for i in np.random.RandomState(seed).permutation(count)]


def _exchange(x, axis, order):
    plain = order == sorted(order)
    groups = None if plain else [order]
    return lax.all_to_all(x, axis, 0, 0, tiled=True, axis_index_groups=groups)


def _dot(a, b, ca, cb, **kw):
    return lax.dot_general(
        a, b, (((ca,), (cb,)), ((), ())), preferred_element_type=F32, **kw
    )


def _splits(total, step):
    return [(lo, min(lo + step, total)) for lo in range(0, total, step)]


def factor_kernel(
    stores,
    step,
    store_order,
    x_hbm,
    gate_hbm,
    up_hbm,
    dh_hbm,
    dy_hbm,
    pmi_hbm,
    phi_hbm,
    pho_hbm,
    pmo_hbm,
    out_ref,
    x,
    gate,
    up,
    dh,
    dy,
    pmi,
    phi,
    pho,
    pmo,
    hidden,
    gate_grad,
    up_grad,
    sems,
):
    features, tokens = gate.shape
    rank = phi.shape[0]
    rows = rank // stores
    seq_len = out_ref.shape[2]
    spans = _splits(features, step)
    model = [
        pltpu.make_async_copy(src, dst, sems.at[i])
        for i, (src, dst) in enumerate(
            [(x_hbm, x), (pmi_hbm, pmi), (dy_hbm, dy), (pmo_hbm, pmo), (phi_hbm, phi), (pho_hbm, pho)]
        )
    ]
    parts = [
        [
            pltpu.make_async_copy(
                src.at[pl.ds(lo, hi - lo)], dst.at[pl.ds(lo, hi - lo)], sems.at[6 + 3 * n + i]
            )
            for i, (src, dst) in enumerate([(gate_hbm, gate), (up_hbm, up), (dh_hbm, dh)])
        ]
        for n, (lo, hi) in enumerate(spans)
    ]
    for copy in model + parts[0]:
        copy.start()
    for part in parts[1:]:
        for copy in part:
            copy.start()

    for copy in model[:4]:
        copy.wait()
    from_model = _dot(x[...], pmi[...], 1, 0).T
    out_two = _dot(pmo[...], dy[...], 1, 1)
    for copy in model[4:]:
        copy.wait()
    in_two = out_zero = out_one = None
    for n, (lo, hi) in enumerate(spans):
        for copy in parts[n]:
            copy.wait()
        block = 64

        def body(i, carry, lo=lo):
            at = pl.ds(pl.multiple_of(lo + i * block, block), block)
            g = gate[at].astype(F32)
            u = up[at].astype(F32)
            d = dh[at].astype(F32)
            sigma = 0.5 * jnp.tanh(0.5 * g) + 0.5
            silu = g * sigma
            hidden[at] = (silu * u).astype(BF)
            up_grad[at] = (d * silu).astype(BF)
            gate_grad[at] = (d * u * (sigma + silu * (1.0 - sigma))).astype(BF)
            return carry

        lax.fori_loop(0, (hi - lo) // block, body, 0, unroll=True)
        a = _dot(phi[:, lo:hi], hidden[lo:hi], 1, 0)
        b = _dot(pho[lo:hi, :rank], gate_grad[lo:hi], 0, 0)
        c = _dot(pho[lo:hi, rank:], up_grad[lo:hi], 0, 0)
        in_two = a if in_two is None else in_two + a
        out_zero = b if out_zero is None else out_zero + b
        out_one = c if out_one is None else out_one + c

    out_all = [out_zero, out_one, out_two]
    for e in range(2):
        at = slice(e * seq_len, (e + 1) * seq_len)
        factors = jnp.concatenate([from_model[:, at], in_two[:, at]], axis=0).astype(BF)
        for s in range(e, stores, 2):
            place = store_order.index(s)
            out_ref[place, : 3 * rank] = factors
            for m in range(3):
                mine = out_all[m][s * rows : (s + 1) * rows, at]
                other = out_all[m][(s ^ 1) * rows : ((s ^ 1) + 1) * rows, at]
                lo = 3 * rank + m * 2 * rows
                out_ref[place, lo : lo + 2 * rows] = jnp.concatenate([mine, other], axis=0).astype(BF)


def sketch_kernel(scale, got, weights, chooser, other, out_ref, total):
    stores = got.shape[0]
    acc = got[0].astype(F32)
    for s in range(1, stores):
        acc = acc + got[s].astype(F32)
    total[...] = acc
    rank = 64
    blocks = []
    for m in range(3):
        lo = 3 * rank + m * 16
        factor = total[m * rank : (m + 1) * rank]
        picked = [total[pl.ds(lo + parity, 8, stride=2)] for parity in range(2)]
        picked = jnp.concatenate(picked, axis=0) * weights[...]
        both = _dot(picked, factor, 1, 1, precision=lax.Precision.HIGHEST)
        blocks.append(jnp.concatenate([both[:8], both[8:]], axis=1))
    sketch = (jnp.concatenate(blocks, axis=0) * scale).astype(BF)

    def body(i, carry):
        out_ref[i] = sketch
        return carry

    lax.fori_loop(0, out_ref.shape[0], body, 0, unroll=8)


def score_kernel(places, gathered, mine, other, chooser, scores, kept, passed, wide):
    groups, lines, lanes = gathered.shape
    capacity = kept.shape[1]
    for i, place in enumerate(places):
        wide[place * lines : (place + 1) * lines] = gathered[i].astype(F32)
    acc = None
    for m in range(3):
        for h, (query, held) in enumerate(((mine, kept), (other, passed))):
            cols = [wide[pl.ds(m * 8 + h * 4 + p, groups, stride=lines)] for p in range(4)]
            block = jnp.concatenate(cols, axis=1).astype(BF)
            term = _dot(block, query[m], 1, 1)
            acc = term if acc is None else acc + term
            held[m] = _dot(chooser[...], block, 1, 0)[:capacity].astype(BF)
    scores[...] = acc


def finish_kernel(store_order, parts, own, received, scores, stored):
    per_core = []
    for core in range(2):
        first, *others = [i for i, s in enumerate(store_order) if s % 2 == core]
        total = parts[first]
        for i in others:
            total = total + parts[i]
        per_core.append(total)
    for z in range(per_core[0].shape[0]):
        for core in range(2):
            scores[2 * z + core : 2 * z + core + 1] = per_core[core][z : z + 1]
    for m in range(3):
        stored[m] = (own[m].astype(F32) + received[m].astype(F32)).astype(BF)


def _vmem(n):
    return [pl.BlockSpec(memory_space=pltpu.VMEM)] * n


def local(
    layer_input,
    gate_pre,
    up_pre,
    hidden_grad,
    out_grad,
    proj_model_in,
    proj_hidden_in,
    proj_hidden_out,
    proj_model_out,
    queries,
    validity,
    owners,
):
    tokens, features = gate_pre.shape
    width = layer_input.shape[1]
    rank = proj_hidden_in.shape[1]
    seq_count, seq_len = validity.shape
    stores = lax.axis_size("store")
    groups = lax.axis_size("fsdp")
    rows = rank // stores
    capacity = 2 * seq_count
    core = lax.axis_index("store") % 2
    store_order = _order(stores, STORE_SEED)
    group_order = _order(groups, GROUP_SEED)

    step = 512
    spans = len(_splits(features, step))
    lines = 3 * rank + 3 * 2 * rows
    send = pl.pallas_call(
        functools.partial(factor_kernel, stores, step, store_order),
        out_shape=jax.ShapeDtypeStruct((stores, lines, seq_len), BF),
        in_specs=[pl.BlockSpec(memory_space=pl.ANY)] * 9,
        out_specs=pl.BlockSpec(memory_space=pltpu.VMEM),
        scratch_shapes=[
            pltpu.VMEM((tokens, width), BF),
            pltpu.VMEM((features, tokens), BF),
            pltpu.VMEM((features, tokens), BF),
            pltpu.VMEM((features, tokens), BF),
            pltpu.VMEM((tokens, width), BF),
            pltpu.VMEM((width, 2 * rank), BF),
            pltpu.VMEM((rank, features), BF),
            pltpu.VMEM((features, 2 * rank), BF),
            pltpu.VMEM((rank, width), BF),
            pltpu.VMEM((features, tokens), BF),
            pltpu.VMEM((features, tokens), BF),
            pltpu.VMEM((features, tokens), BF),
            pltpu.SemaphoreType.DMA((6 + 3 * spans,)),
        ],
        compiler_params=pltpu.CompilerParams(vmem_limit_bytes=60 * 2**20),
        name="factors",
    )(
        layer_input,
        gate_pre.T,
        up_pre.T,
        hidden_grad.T,
        out_grad,
        proj_model_in,
        proj_hidden_in.T,
        proj_hidden_out,
        proj_model_out.T,
    )
    got = _exchange(send, "store", store_order)

    share = groups // stores
    places = [store_order.index(g // share) * share + g % share for g in group_order]
    at_place = np.argsort([store_order.index(g // share) * share + g % share for g in range(groups)])
    own_index = lax.axis_index("fsdp")
    mine = (owners == own_index).astype(jnp.int32)
    count = owners.shape[0]
    first = lax.broadcasted_iota(jnp.int32, (count, count), 0)
    second = lax.broadcasted_iota(jnp.int32, (count, count), 1)
    slot_rank = jnp.sum(jnp.where(first < second, mine[:, None], 0), axis=0)
    slots = jnp.arange(8, dtype=jnp.int32)
    hit = ((slot_rank[None, :] == slots[:, None]) & (mine[None, :] == 1)).astype(BF)
    wanted = jnp.asarray(seq_count * at_place.astype(np.int32)) + core
    chooser = jnp.dot(
        hit,
        (jnp.arange(count, dtype=jnp.int32)[:, None] == wanted[None, :]).astype(BF),
        preferred_element_type=F32,
    ).astype(BF)

    flip = [(s, s ^ 1) for s in range(stores)]
    query_rows = queries.transpose(1, 0, 2)
    other_rows = lax.ppermute(query_rows, "store", flip)
    weights = jnp.where(core == 0, validity[0], validity[1]).astype(F32).reshape(1, seq_len)
    lines = 3 * 2 * rows * rank // 128
    spread = pl.pallas_call(
        functools.partial(sketch_kernel, float(seq_len) ** (-0.5)),
        out_shape=jax.ShapeDtypeStruct((groups, lines, 128), BF),
        in_specs=_vmem(2) + [pl.BlockSpec(memory_space=pl.ANY)] * 2,
        out_specs=pl.BlockSpec(memory_space=pltpu.VMEM),
        scratch_shapes=[pltpu.VMEM(got.shape[1:], F32)],
        compiler_params=pltpu.CompilerParams(vmem_limit_bytes=8 * 2**20),
        name="sketch",
    )(got, weights, chooser, other_rows)
    gathered = _exchange(spread, "fsdp", group_order)

    query_count = queries.shape[0]
    held = jax.ShapeDtypeStruct((3, capacity, rows * rank), BF)
    partial_scores, kept, passed = pl.pallas_call(
        functools.partial(score_kernel, places),
        out_shape=(jax.ShapeDtypeStruct((groups, query_count), F32), held, held),
        in_specs=_vmem(4),
        out_specs=tuple(_vmem(3)),
        scratch_shapes=[pltpu.VMEM((groups * lines, 128), F32)],
        compiler_params=pltpu.CompilerParams(vmem_limit_bytes=12 * 2**20),
        name="scores",
    )(gathered, query_rows, other_rows, chooser)

    parts = _exchange(
        partial_scores.reshape(stores, share, query_count), "store", store_order
    )
    received = lax.ppermute(passed, "store", flip)
    scores, stored = pl.pallas_call(
        functools.partial(finish_kernel, store_order),
        out_shape=(
            jax.ShapeDtypeStruct((2 * groups // stores, query_count), F32),
            held,
        ),
        in_specs=_vmem(3),
        out_specs=tuple(_vmem(2)),
        compiler_params=pltpu.CompilerParams(vmem_limit_bytes=8 * 2**20),
        name="finish",
    )(parts, kept, received)
    stored = stored.transpose(1, 0, 2)
    return (scores, stored)


def solution(mesh):
    placed = (
        P("fsdp", "store"),
        P("fsdp", "store"),
        P("fsdp", "store"),
        P("fsdp", "store"),
        P("fsdp", "store"),
        P("store", None),
        P("store", None),
        P("store", None),
        P("store", None),
        P("fsdp", None, "store"),
        P("fsdp", None),
        P(),
    )
    return jax.shard_map(
        local,
        mesh=mesh,
        in_specs=placed,
        out_specs=(P("store", "fsdp"), P("fsdp", None, "store")),
        check_vma=False,
    )
```

```python
import functools

import jax
import jax.numpy as jnp
import numpy as np
from jax import lax
from jax.experimental import pallas as pl
from jax.experimental.pallas import tpu as pltpu
from jax.sharding import PartitionSpec as P

BF = jnp.bfloat16
F32 = jnp.float32
GROUP_SEED = 29
STORE_SEED = 8


def _order(count, seed):
    if seed is None:
        return list(range(count))
    return [int(i) for i in np.random.RandomState(seed).permutation(count)]


def _exchange(x, axis, order):
    plain = order == sorted(order)
    groups = None if plain else [order]
    return lax.all_to_all(x, axis, 0, 0, tiled=True, axis_index_groups=groups)


def _dot(a, b, ca, cb, **kw):
    return lax.dot_general(
        a, b, (((ca,), (cb,)), ((), ())), preferred_element_type=F32, **kw
    )


def _splits(total, step):
    return [(lo, min(lo + step, total)) for lo in range(0, total, step)]


def factor_kernel(
    stores,
    step,
    store_order,
    x_hbm,
    gate_hbm,
    up_hbm,
    dh_hbm,
    dy_hbm,
    pmi_hbm,
    phi_hbm,
    pho_hbm,
    pmo_hbm,
    out_ref,
    x,
    gate,
    up,
    dh,
    dy,
    pmi,
    phi,
    pho,
    pmo,
    hidden,
    gate_grad,
    up_grad,
    sems,
):
    features, tokens = gate.shape
    rank = phi.shape[0]
    rows = rank // stores
    seq_len = out_ref.shape[2]
    spans = _splits(features, step)
    model = [
        pltpu.make_async_copy(src, dst, sems.at[i])
        for i, (src, dst) in enumerate(
            [(x_hbm, x), (pmi_hbm, pmi), (dy_hbm, dy), (pmo_hbm, pmo), (phi_hbm, phi), (pho_hbm, pho)]
        )
    ]
    parts = [
        [
            pltpu.make_async_copy(
                src.at[pl.ds(lo, hi - lo)], dst.at[pl.ds(lo, hi - lo)], sems.at[6 + 3 * n + i]
            )
            for i, (src, dst) in enumerate([(gate_hbm, gate), (up_hbm, up), (dh_hbm, dh)])
        ]
        for n, (lo, hi) in enumerate(spans)
    ]
    for copy in model + parts[0]:
        copy.start()
    for part in parts[1:]:
        for copy in part:
            copy.start()

    for copy in model[:4]:
        copy.wait()
    from_model = _dot(x[...], pmi[...], 1, 0).T
    out_two = _dot(pmo[...], dy[...], 1, 1)
    for copy in model[4:]:
        copy.wait()
    in_two = out_zero = out_one = None
    for n, (lo, hi) in enumerate(spans):
        for copy in parts[n]:
            copy.wait()
        block = 64

        def body(i, carry, lo=lo):
            at = pl.ds(pl.multiple_of(lo + i * block, block), block)
            g = gate[at].astype(F32)
            u = up[at].astype(F32)
            d = dh[at].astype(F32)
            sigma = 0.5 * jnp.tanh(0.5 * g) + 0.5
            silu = g * sigma
            hidden[at] = (silu * u).astype(BF)
            up_grad[at] = (d * silu).astype(BF)
            gate_grad[at] = (d * u * (sigma + silu * (1.0 - sigma))).astype(BF)
            return carry

        lax.fori_loop(0, (hi - lo) // block, body, 0, unroll=True)
        a = _dot(phi[:, lo:hi], hidden[lo:hi], 1, 0)
        b = _dot(pho[lo:hi, :rank], gate_grad[lo:hi], 0, 0)
        c = _dot(pho[lo:hi, rank:], up_grad[lo:hi], 0, 0)
        in_two = a if in_two is None else in_two + a
        out_zero = b if out_zero is None else out_zero + b
        out_one = c if out_one is None else out_one + c

    out_all = [out_zero, out_one, out_two]
    for e in range(2):
        at = slice(e * seq_len, (e + 1) * seq_len)
        factors = jnp.concatenate([from_model[:, at], in_two[:, at]], axis=0).astype(BF)
        for s in range(e, stores, 2):
            place = store_order.index(s)
            out_ref[place, : 3 * rank] = factors
            for m in range(3):
                mine = out_all[m][s * rows : (s + 1) * rows, at]
                other = out_all[m][(s ^ 1) * rows : ((s ^ 1) + 1) * rows, at]
                lo = 3 * rank + m * 2 * rows
                out_ref[place, lo : lo + 2 * rows] = jnp.concatenate([mine, other], axis=0).astype(BF)


def sketch_kernel(scale, got, weights, chooser, other, out_ref, total):
    stores = got.shape[0]
    acc = got[0].astype(F32)
    for s in range(1, stores):
        acc = acc + got[s].astype(F32)
    total[...] = acc
    rank = 64
    blocks = []
    for m in range(3):
        lo = 3 * rank + m * 16
        factor = total[m * rank : (m + 1) * rank]
        picked = [total[pl.ds(lo + parity, 8, stride=2)] for parity in range(2)]
        picked = jnp.concatenate(picked, axis=0) * weights[...]
        both = _dot(picked, factor, 1, 1, precision=lax.Precision.HIGHEST)
        blocks.append(jnp.concatenate([both[:8], both[8:]], axis=1))
    sketch = (jnp.concatenate(blocks, axis=0) * scale).astype(BF)

    def body(i, carry):
        out_ref[i] = sketch
        return carry

    lax.fori_loop(0, out_ref.shape[0], body, 0, unroll=8)


def score_kernel(places, gathered, mine, other, chooser, scores, kept, passed, wide):
    groups, lines, lanes = gathered.shape
    capacity = kept.shape[1]
    for i, place in enumerate(places):
        wide[place * lines : (place + 1) * lines] = gathered[i].astype(F32)
    acc = None
    for m in range(3):
        for h, (query, held) in enumerate(((mine, kept), (other, passed))):
            cols = [wide[pl.ds(m * 8 + h * 4 + p, groups, stride=lines)] for p in range(4)]
            block = jnp.concatenate(cols, axis=1).astype(BF)
            term = _dot(block, query[m], 1, 1)
            acc = term if acc is None else acc + term
            held[m] = _dot(chooser[...], block, 1, 0)[:capacity].astype(BF)
    scores[...] = acc


def finish_kernel(store_order, parts, own, received, scores, stored):
    per_core = []
    for core in range(2):
        first, *others = [i for i, s in enumerate(store_order) if s % 2 == core]
        total = parts[first]
        for i in others:
            total = total + parts[i]
        per_core.append(total)
    for z in range(per_core[0].shape[0]):
        for core in range(2):
            scores[2 * z + core : 2 * z + core + 1] = per_core[core][z : z + 1]
    for m in range(3):
        stored[m] = (own[m].astype(F32) + received[m].astype(F32)).astype(BF)


def _vmem(n):
    return [pl.BlockSpec(memory_space=pltpu.VMEM)] * n


def local(
    layer_input,
    gate_pre,
    up_pre,
    hidden_grad,
    out_grad,
    proj_model_in,
    proj_hidden_in,
    proj_hidden_out,
    proj_model_out,
    queries,
    validity,
    owners,
):
    tokens, features = gate_pre.shape
    width = layer_input.shape[1]
    rank = proj_hidden_in.shape[1]
    seq_count, seq_len = validity.shape
    stores = lax.axis_size("store")
    groups = lax.axis_size("fsdp")
    rows = rank // stores
    capacity = 2 * seq_count
    core = lax.axis_index("store") % 2
    store_order = _order(stores, STORE_SEED)
    group_order = _order(groups, GROUP_SEED)

    step = 512
    spans = len(_splits(features, step))
    lines = 3 * rank + 3 * 2 * rows
    send = pl.pallas_call(
        functools.partial(factor_kernel, stores, step, store_order),
        out_shape=jax.ShapeDtypeStruct((stores, lines, seq_len), BF),
        in_specs=[pl.BlockSpec(memory_space=pl.ANY)] * 9,
        out_specs=pl.BlockSpec(memory_space=pltpu.VMEM),
        scratch_shapes=[
            pltpu.VMEM((tokens, width), BF),
            pltpu.VMEM((features, tokens), BF),
            pltpu.VMEM((features, tokens), BF),
            pltpu.VMEM((features, tokens), BF),
            pltpu.VMEM((tokens, width), BF),
            pltpu.VMEM((width, 2 * rank), BF),
            pltpu.VMEM((rank, features), BF),
            pltpu.VMEM((features, 2 * rank), BF),
            pltpu.VMEM((rank, width), BF),
            pltpu.VMEM((features, tokens), BF),
            pltpu.VMEM((features, tokens), BF),
            pltpu.VMEM((features, tokens), BF),
            pltpu.SemaphoreType.DMA((6 + 3 * spans,)),
        ],
        compiler_params=pltpu.CompilerParams(vmem_limit_bytes=60 * 2**20),
        name="factors",
    )(
        layer_input,
        gate_pre.T,
        up_pre.T,
        hidden_grad.T,
        out_grad,
        proj_model_in,
        proj_hidden_in.T,
        proj_hidden_out,
        proj_model_out.T,
    )
    got = _exchange(send, "store", store_order)

    share = groups // stores
    places = [store_order.index(g // share) * share + g % share for g in group_order]
    at_place = np.argsort([store_order.index(g // share) * share + g % share for g in range(groups)])
    own_index = lax.axis_index("fsdp")
    mine = (owners == own_index).astype(jnp.int32)
    count = owners.shape[0]
    first = lax.broadcasted_iota(jnp.int32, (count, count), 0)
    second = lax.broadcasted_iota(jnp.int32, (count, count), 1)
    slot_rank = jnp.sum(jnp.where(first < second, mine[:, None], 0), axis=0)
    slots = jnp.arange(8, dtype=jnp.int32)
    hit = ((slot_rank[None, :] == slots[:, None]) & (mine[None, :] == 1)).astype(BF)
    wanted = jnp.asarray(seq_count * at_place.astype(np.int32)) + core
    chooser = jnp.dot(
        hit,
        (jnp.arange(count, dtype=jnp.int32)[:, None] == wanted[None, :]).astype(BF),
        preferred_element_type=F32,
    ).astype(BF)

    flip = [(s, s ^ 1) for s in range(stores)]
    query_rows = queries.transpose(1, 0, 2)
    other_rows = lax.ppermute(query_rows, "store", flip)
    weights = jnp.where(core == 0, validity[0], validity[1]).astype(F32).reshape(1, seq_len)
    lines = 3 * 2 * rows * rank // 128
    spread = pl.pallas_call(
        functools.partial(sketch_kernel, float(seq_len) ** (-0.5)),
        out_shape=jax.ShapeDtypeStruct((groups, lines, 128), BF),
        in_specs=_vmem(2) + [pl.BlockSpec(memory_space=pl.ANY)] * 2,
        out_specs=pl.BlockSpec(memory_space=pltpu.VMEM),
        scratch_shapes=[pltpu.VMEM(got.shape[1:], F32)],
        compiler_params=pltpu.CompilerParams(vmem_limit_bytes=8 * 2**20),
        name="sketch",
    )(got, weights, chooser, other_rows)
    gathered = _exchange(spread, "fsdp", group_order)

    query_count = queries.shape[0]
    held = jax.ShapeDtypeStruct((3, capacity, rows * rank), BF)
    partial_scores, kept, passed = pl.pallas_call(
        functools.partial(score_kernel, places),
        out_shape=(jax.ShapeDtypeStruct((groups, query_count), F32), held, held),
        in_specs=_vmem(4),
        out_specs=tuple(_vmem(3)),
        scratch_shapes=[pltpu.VMEM((groups * lines, 128), F32)],
        compiler_params=pltpu.CompilerParams(vmem_limit_bytes=12 * 2**20),
        name="scores",
    )(gathered, query_rows, other_rows, chooser)

    parts = _exchange(
        partial_scores.reshape(stores, share, query_count), "store", store_order
    )
    received = lax.ppermute(passed, "store", flip)
    scores, stored = pl.pallas_call(
        functools.partial(finish_kernel, store_order),
        out_shape=(
            jax.ShapeDtypeStruct((2 * groups // stores, query_count), F32),
            held,
        ),
        in_specs=_vmem(3),
        out_specs=tuple(_vmem(2)),
        compiler_params=pltpu.CompilerParams(vmem_limit_bytes=8 * 2**20),
        name="finish",
    )(parts, kept, received)
    stored = stored.transpose(1, 0, 2)
    return (scores, stored)


def solution(mesh):
    placed = (
        P("fsdp", "store"),
        P("fsdp", "store"),
        P("fsdp", "store"),
        P("fsdp", "store"),
        P("fsdp", "store"),
        P("store", None),
        P("store", None),
        P("store", None),
        P("store", None),
        P("fsdp", None, "store"),
        P("fsdp", None),
        P(),
    )
    return jax.shard_map(
        local,
        mesh=mesh,
        in_specs=placed,
        out_specs=(P("store", "fsdp"), P("fsdp", None, "store")),
        check_vma=False,
    )
```

```python
import functools

import jax
import jax.numpy as jnp
import numpy as np
from jax import lax
from jax.experimental import pallas as pl
from jax.experimental.pallas import tpu as pltpu
from jax.sharding import PartitionSpec as P

BF = jnp.bfloat16
F32 = jnp.float32
GROUP_SEED = 29
STORE_SEED = 9


def _order(count, seed):
    if seed is None:
        return list(range(count))
    return [int(i) for i in np.random.RandomState(seed).permutation(count)]


def _exchange(x, axis, order):
    plain = order == sorted(order)
    groups = None if plain else [order]
    return lax.all_to_all(x, axis, 0, 0, tiled=True, axis_index_groups=groups)


def _dot(a, b, ca, cb, **kw):
    return lax.dot_general(
        a, b, (((ca,), (cb,)), ((), ())), preferred_element_type=F32, **kw
    )


def _splits(total, step):
    return [(lo, min(lo + step, total)) for lo in range(0, total, step)]


def factor_kernel(
    stores,
    step,
    store_order,
    x_hbm,
    gate_hbm,
    up_hbm,
    dh_hbm,
    dy_hbm,
    pmi_hbm,
    phi_hbm,
    pho_hbm,
    pmo_hbm,
    out_ref,
    x,
    gate,
    up,
    dh,
    dy,
    pmi,
    phi,
    pho,
    pmo,
    hidden,
    gate_grad,
    up_grad,
    sems,
):
    features, tokens = gate.shape
    rank = phi.shape[0]
    rows = rank // stores
    seq_len = out_ref.shape[2]
    spans = _splits(features, step)
    model = [
        pltpu.make_async_copy(src, dst, sems.at[i])
        for i, (src, dst) in enumerate(
            [(x_hbm, x), (pmi_hbm, pmi), (dy_hbm, dy), (pmo_hbm, pmo), (phi_hbm, phi), (pho_hbm, pho)]
        )
    ]
    parts = [
        [
            pltpu.make_async_copy(
                src.at[pl.ds(lo, hi - lo)], dst.at[pl.ds(lo, hi - lo)], sems.at[6 + 3 * n + i]
            )
            for i, (src, dst) in enumerate([(gate_hbm, gate), (up_hbm, up), (dh_hbm, dh)])
        ]
        for n, (lo, hi) in enumerate(spans)
    ]
    for copy in model + parts[0]:
        copy.start()
    for part in parts[1:]:
        for copy in part:
            copy.start()

    for copy in model[:4]:
        copy.wait()
    from_model = _dot(x[...], pmi[...], 1, 0).T
    out_two = _dot(pmo[...], dy[...], 1, 1)
    for copy in model[4:]:
        copy.wait()
    in_two = out_zero = out_one = None
    for n, (lo, hi) in enumerate(spans):
        for copy in parts[n]:
            copy.wait()
        block = 64

        def body(i, carry, lo=lo):
            at = pl.ds(pl.multiple_of(lo + i * block, block), block)
            g = gate[at].astype(F32)
            u = up[at].astype(F32)
            d = dh[at].astype(F32)
            sigma = 0.5 * jnp.tanh(0.5 * g) + 0.5
            silu = g * sigma
            hidden[at] = (silu * u).astype(BF)
            up_grad[at] = (d * silu).astype(BF)
            gate_grad[at] = (d * u * (sigma + silu * (1.0 - sigma))).astype(BF)
            return carry

        lax.fori_loop(0, (hi - lo) // block, body, 0, unroll=True)
        a = _dot(phi[:, lo:hi], hidden[lo:hi], 1, 0)
        b = _dot(pho[lo:hi, :rank], gate_grad[lo:hi], 0, 0)
        c = _dot(pho[lo:hi, rank:], up_grad[lo:hi], 0, 0)
        in_two = a if in_two is None else in_two + a
        out_zero = b if out_zero is None else out_zero + b
        out_one = c if out_one is None else out_one + c

    out_all = [out_zero, out_one, out_two]
    for e in range(2):
        at = slice(e * seq_len, (e + 1) * seq_len)
        factors = jnp.concatenate([from_model[:, at], in_two[:, at]], axis=0).astype(BF)
        for s in range(e, stores, 2):
            place = store_order.index(s)
            out_ref[place, : 3 * rank] = factors
            for m in range(3):
                mine = out_all[m][s * rows : (s + 1) * rows, at]
                other = out_all[m][(s ^ 1) * rows : ((s ^ 1) + 1) * rows, at]
                lo = 3 * rank + m * 2 * rows
                out_ref[place, lo : lo + 2 * rows] = jnp.concatenate([mine, other], axis=0).astype(BF)


def sketch_kernel(scale, got, weights, chooser, other, out_ref, total):
    stores = got.shape[0]
    acc = got[0].astype(F32)
    for s in range(1, stores):
        acc = acc + got[s].astype(F32)
    total[...] = acc
    rank = 64
    blocks = []
    for m in range(3):
        lo = 3 * rank + m * 16
        factor = total[m * rank : (m + 1) * rank]
        picked = [total[pl.ds(lo + parity, 8, stride=2)] for parity in range(2)]
        picked = jnp.concatenate(picked, axis=0) * weights[...]
        both = _dot(picked, factor, 1, 1, precision=lax.Precision.HIGHEST)
        blocks.append(jnp.concatenate([both[:8], both[8:]], axis=1))
    sketch = (jnp.concatenate(blocks, axis=0) * scale).astype(BF)

    def body(i, carry):
        out_ref[i] = sketch
        return carry

    lax.fori_loop(0, out_ref.shape[0], body, 0, unroll=8)


def score_kernel(places, gathered, mine, other, chooser, scores, kept, passed, wide):
    groups, lines, lanes = gathered.shape
    capacity = kept.shape[1]
    for i, place in enumerate(places):
        wide[place * lines : (place + 1) * lines] = gathered[i].astype(F32)
    acc = None
    for m in range(3):
        for h, (query, held) in enumerate(((mine, kept), (other, passed))):
            cols = [wide[pl.ds(m * 8 + h * 4 + p, groups, stride=lines)] for p in range(4)]
            block = jnp.concatenate(cols, axis=1).astype(BF)
            term = _dot(block, query[m], 1, 1)
            acc = term if acc is None else acc + term
            held[m] = _dot(chooser[...], block, 1, 0)[:capacity].astype(BF)
    scores[...] = acc


def finish_kernel(store_order, parts, own, received, scores, stored):
    per_core = []
    for core in range(2):
        first, *others = [i for i, s in enumerate(store_order) if s % 2 == core]
        total = parts[first]
        for i in others:
            total = total + parts[i]
        per_core.append(total)
    for z in range(per_core[0].shape[0]):
        for core in range(2):
            scores[2 * z + core : 2 * z + core + 1] = per_core[core][z : z + 1]
    for m in range(3):
        stored[m] = (own[m].astype(F32) + received[m].astype(F32)).astype(BF)


def _vmem(n):
    return [pl.BlockSpec(memory_space=pltpu.VMEM)] * n


def local(
    layer_input,
    gate_pre,
    up_pre,
    hidden_grad,
    out_grad,
    proj_model_in,
    proj_hidden_in,
    proj_hidden_out,
    proj_model_out,
    queries,
    validity,
    owners,
):
    tokens, features = gate_pre.shape
    width = layer_input.shape[1]
    rank = proj_hidden_in.shape[1]
    seq_count, seq_len = validity.shape
    stores = lax.axis_size("store")
    groups = lax.axis_size("fsdp")
    rows = rank // stores
    capacity = 2 * seq_count
    core = lax.axis_index("store") % 2
    store_order = _order(stores, STORE_SEED)
    group_order = _order(groups, GROUP_SEED)

    step = 512
    spans = len(_splits(features, step))
    lines = 3 * rank + 3 * 2 * rows
    send = pl.pallas_call(
        functools.partial(factor_kernel, stores, step, store_order),
        out_shape=jax.ShapeDtypeStruct((stores, lines, seq_len), BF),
        in_specs=[pl.BlockSpec(memory_space=pl.ANY)] * 9,
        out_specs=pl.BlockSpec(memory_space=pltpu.VMEM),
        scratch_shapes=[
            pltpu.VMEM((tokens, width), BF),
            pltpu.VMEM((features, tokens), BF),
            pltpu.VMEM((features, tokens), BF),
            pltpu.VMEM((features, tokens), BF),
            pltpu.VMEM((tokens, width), BF),
            pltpu.VMEM((width, 2 * rank), BF),
            pltpu.VMEM((rank, features), BF),
            pltpu.VMEM((features, 2 * rank), BF),
            pltpu.VMEM((rank, width), BF),
            pltpu.VMEM((features, tokens), BF),
            pltpu.VMEM((features, tokens), BF),
            pltpu.VMEM((features, tokens), BF),
            pltpu.SemaphoreType.DMA((6 + 3 * spans,)),
        ],
        compiler_params=pltpu.CompilerParams(vmem_limit_bytes=60 * 2**20),
        name="factors",
    )(
        layer_input,
        gate_pre.T,
        up_pre.T,
        hidden_grad.T,
        out_grad,
        proj_model_in,
        proj_hidden_in.T,
        proj_hidden_out,
        proj_model_out.T,
    )
    got = _exchange(send, "store", store_order)

    share = groups // stores
    places = [store_order.index(g // share) * share + g % share for g in group_order]
    at_place = np.argsort([store_order.index(g // share) * share + g % share for g in range(groups)])
    own_index = lax.axis_index("fsdp")
    mine = (owners == own_index).astype(jnp.int32)
    count = owners.shape[0]
    first = lax.broadcasted_iota(jnp.int32, (count, count), 0)
    second = lax.broadcasted_iota(jnp.int32, (count, count), 1)
    slot_rank = jnp.sum(jnp.where(first < second, mine[:, None], 0), axis=0)
    slots = jnp.arange(8, dtype=jnp.int32)
    hit = ((slot_rank[None, :] == slots[:, None]) & (mine[None, :] == 1)).astype(BF)
    wanted = jnp.asarray(seq_count * at_place.astype(np.int32)) + core
    chooser = jnp.dot(
        hit,
        (jnp.arange(count, dtype=jnp.int32)[:, None] == wanted[None, :]).astype(BF),
        preferred_element_type=F32,
    ).astype(BF)

    flip = [(s, s ^ 1) for s in range(stores)]
    query_rows = queries.transpose(1, 0, 2)
    other_rows = lax.ppermute(query_rows, "store", flip)
    weights = jnp.where(core == 0, validity[0], validity[1]).astype(F32).reshape(1, seq_len)
    lines = 3 * 2 * rows * rank // 128
    spread = pl.pallas_call(
        functools.partial(sketch_kernel, float(seq_len) ** (-0.5)),
        out_shape=jax.ShapeDtypeStruct((groups, lines, 128), BF),
        in_specs=_vmem(2) + [pl.BlockSpec(memory_space=pl.ANY)] * 2,
        out_specs=pl.BlockSpec(memory_space=pltpu.VMEM),
        scratch_shapes=[pltpu.VMEM(got.shape[1:], F32)],
        compiler_params=pltpu.CompilerParams(vmem_limit_bytes=8 * 2**20),
        name="sketch",
    )(got, weights, chooser, other_rows)
    gathered = _exchange(spread, "fsdp", group_order)

    query_count = queries.shape[0]
    held = jax.ShapeDtypeStruct((3, capacity, rows * rank), BF)
    partial_scores, kept, passed = pl.pallas_call(
        functools.partial(score_kernel, places),
        out_shape=(jax.ShapeDtypeStruct((groups, query_count), F32), held, held),
        in_specs=_vmem(4),
        out_specs=tuple(_vmem(3)),
        scratch_shapes=[pltpu.VMEM((groups * lines, 128), F32)],
        compiler_params=pltpu.CompilerParams(vmem_limit_bytes=12 * 2**20),
        name="scores",
    )(gathered, query_rows, other_rows, chooser)

    parts = _exchange(
        partial_scores.reshape(stores, share, query_count), "store", store_order
    )
    received = lax.ppermute(passed, "store", flip)
    scores, stored = pl.pallas_call(
        functools.partial(finish_kernel, store_order),
        out_shape=(
            jax.ShapeDtypeStruct((2 * groups // stores, query_count), F32),
            held,
        ),
        in_specs=_vmem(3),
        out_specs=tuple(_vmem(2)),
        compiler_params=pltpu.CompilerParams(vmem_limit_bytes=8 * 2**20),
        name="finish",
    )(parts, kept, received)
    stored = stored.transpose(1, 0, 2)
    return (scores, stored)


def solution(mesh):
    placed = (
        P("fsdp", "store"),
        P("fsdp", "store"),
        P("fsdp", "store"),
        P("fsdp", "store"),
        P("fsdp", "store"),
        P("store", None),
        P("store", None),
        P("store", None),
        P("store", None),
        P("fsdp", None, "store"),
        P("fsdp", None),
        P(),
    )
    return jax.shard_map(
        local,
        mesh=mesh,
        in_specs=placed,
        out_specs=(P("store", "fsdp"), P("fsdp", None, "store")),
        check_vma=False,
    )
```
